32 devices in a mesh: row: 8 (over z, y), col: 4 (over x, core).
Axes of the slice: x: 2, y: 2, z: 4, core: 2. Of those that a mesh axis runs over, the one named last changes fastest.
Arguments:
- hidden: bfloat16 [128, 28672], P('col', 'row'), may hold values from -6 to 6
- down_weight: bfloat16 [28672, 8192], P('row', 'col'), may hold values from -0.03125 to 0.03125
- out_grad: bfloat16 [128, 8192], P('row', 'col'), may hold values from -6 to 6
Outputs:
- projected: bfloat16 [128, 8192], P('row', 'col')
- hidden_grad: bfloat16 [128, 28672], P('col', 'row')
- weight_grad: float32 [28672, 8192], P('row', 'col')
The draws below stay inside these ranges and needn't reach their ends.
All inputs are finite; a program needn't handle non-finite values.
Results may differ from the reference program's by a relative error of at most 0.001.
Values may be sent and summed in bfloat16 or wider, within the bound.
A program may use at most 128 MiB of HBM per device.

```python
import jax
import jax.numpy as jnp
from jax import lax

D = 8192
FF = 28672
TOKENS = 128


def raised(drawn, own_key, source, target, blocks, factor):
    def block_of(axis_at):
        return (jnp.arange(drawn.shape[axis_at]) // (drawn.shape[axis_at] // blocks)).reshape((-1,) + (1,) * (drawn.ndim - 1 - axis_at))

    near = jax.random.permutation(own_key, blocks)[block_of(target)]
    other_side = (block_of(target) + blocks // 2) % blocks
    return jnp.where((block_of(source) == near) | (block_of(source) == other_side), factor * drawn, drawn)


def levels(key, extent, pieces, least, high):
    loudness, own = 1.0, jax.random.fold_in(key, 6)
    for dim, shards_of in pieces:
        draws = jnp.exp(jax.random.uniform(jax.random.fold_in(own, dim), (shards_of,), jnp.float32, least / len(pieces), high / len(pieces)))
        loudness = loudness * jnp.repeat(draws, extent[dim] // shards_of).reshape([-1 if axis == dim else 1 for axis in range(len(extent))])
    return loudness


def noise(stream_key, dims, width, reach, pieces=(), kind=jnp.bfloat16):
    gain = levels(stream_key, dims, pieces, -0.22, 0.18) if pieces else 1.0
    values = jax.random.normal(stream_key, dims, jnp.float32) * width * gain
    return jnp.minimum(jnp.maximum(values, -reach), reach).astype(kind)


def noise_with(rng, shape, width, reach, pieces, heavy, dtype=jnp.bfloat16):
    values = width * jax.random.normal(rng, shape, jnp.float32)
    if pieces:
        values = values * levels(rng, shape, pieces, -0.22, 0.18)
    return jnp.clip(raised(values, jax.random.fold_in(rng, 3), *heavy), -reach, reach).astype(dtype)


def setup_inputs(seed: int = 0) -> dict:
    key_list = jax.random.split(jax.random.key(seed), 4)
    return {
        "hidden": noise_with(key_list[0], (TOKENS, FF), 1.0, 6.0, ((0, 4), (1, 8)), (1, 0, 8, 2.0)),
        "down_weight": noise(key_list[1], (FF, D), FF ** -0.5, 0.03125, ((0, 8), (1, 4))),
        "out_grad": noise_with(key_list[2], (TOKENS, D), 1.0, 6.0, ((0, 8), (1, 4)), (1, 0, 8, 2.0)),
    }


def reference(hidden, down_weight, out_grad):
    projected = jnp.dot(hidden, down_weight, preferred_element_type=jnp.float32).astype(jnp.bfloat16)
    hidden_grad = lax.dot_general(out_grad, down_weight, (((1,), (1,)), ((), ())), preferred_element_type=jnp.float32).astype(jnp.bfloat16)
    weight_grad = lax.dot_general(hidden, out_grad, (((0,), (0,)), ((), ())), preferred_element_type=jnp.float32)
    weight_grad = weight_grad / jnp.sqrt(jnp.float32(TOKENS))
    return (projected, hidden_grad, weight_grad)
```

```python
import functools

import jax
import jax.numpy as jnp
from jax import lax
from jax.experimental import pallas as pl
from jax.experimental.pallas import tpu as pltpu
from jax.sharding import PartitionSpec as P

MESH = pl.DeviceIdType.MESH


def tile_of(extent, most):
    best = 128
    for width in range(128, most + 1, 128):
        if extent % width == 0:
            best = width
    return best


def exchange_kernel(
    nrow,
    ncol,
    hidden,
    weight,
    grad,
    proj_out,
    hgrad_out,
    all_hidden_out,
    all_grad_out,
    w,
    ah,
    ag,
    p_part,
    p_recv,
    p_recv_z,
    h_part,
    h_recv,
    h_recv_x,
    w_sem,
    own_sem,
    out_sem,
    hx_send,
    hx_recv,
    hc_send,
    hc_recv,
    gz_send,
    gz_recv,
    gy_send,
    gy_recv,
    py_send,
    py_recv,
    pz_send,
    pz_recv,
    qc_send,
    qc_recv,
    qx_send,
    qx_recv,
):
    nz, nx = nrow // 2, ncol // 2
    row, col = lax.axis_index("row"), lax.axis_index("col")
    z, y = row // 2, lax.rem(row, 2)
    x, core = col // 2, lax.rem(col, 2)
    sibling = (row, x * 2 + 1 - core)
    across = (z * 2 + 1 - y, col)

    def x_peer(d):
        return (row, lax.rem(x + d, nx) * 2 + core)

    def z_peer(d):
        return (lax.rem(z + d, nz) * 2 + y, col)

    def remote(src, dst, send, recv, device):
        return pltpu.make_async_remote_copy(
            src_ref=src, dst_ref=dst, send_sem=send, recv_sem=recv, device_id=device, device_id_type=MESH
        )

    hb, ff = hidden.shape
    gb, dd = grad.shape
    pieces = hx_recv.shape[0]
    wide = ff // pieces
    np_, tp = p_part.shape[0], p_part.shape[-1]
    nh, th = h_part.shape[0], h_part.shape[-1]

    w_copies = []
    for t in range(nh):
        rows = pl.ds(t * th, th)
        c = pltpu.make_async_copy(weight.at[rows], w.at[rows], w_sem.at[t])
        c.start()
        w_copies.append(c)

    def h_block(owner):
        return pl.ds(pl.multiple_of(owner * hb, hb), hb)

    def g_block(owner):
        return pl.ds(pl.multiple_of(owner * gb, gb), gb)

    own = [
        pltpu.make_async_copy(hidden, ah.at[h_block(col)], own_sem.at[0]),
        pltpu.make_async_copy(grad, ag.at[g_block(row)], own_sem.at[1]),
    ]
    for c in own:
        c.start()

    barrier = pltpu.get_barrier_semaphore()
    peers = [sibling, across] + [x_peer(d) for d in range(1, nx)] + [z_peer(d) for d in range(1, nz)]
    for peer in peers:
        pl.semaphore_signal(barrier, inc=1, device_id=peer, device_id_type=MESH)
    pl.semaphore_wait(barrier, len(peers))

    sends = []
    for k in range(pieces):
        cols = pl.ds(k * wide, wide)
        for d in range(1, nx):
            c = remote(
                hidden.at[:, cols], ah.at[h_block(col), cols], hx_send.at[k, d - 1], hx_recv.at[k, d - 1], x_peer(d)
            )
            c.start()
            sends.append(c)
    for d in range(1, nz):
        c = remote(grad, ag.at[g_block(row)], gz_send.at[d - 1], gz_recv.at[d - 1], z_peer(d))
        c.start()
        sends.append(c)
    c = remote(grad, ag.at[g_block(row)], gy_send.at[0], gy_recv.at[0], across)
    c.start()
    sends.append(c)
    for k in range(pieces):
        cols = pl.ds(k * wide, wide)
        c = remote(hidden.at[:, cols], ah.at[h_block(col), cols], hc_send.at[k, 0], hc_recv.at[k, 0], sibling)
        c.start()
        sends.append(c)

    for d in range(1, nz):
        source = lax.rem(z + nz - d, nz) * 2 + y
        part = ag.at[g_block(source)]
        remote(part, part, gz_send.at[d - 1], gz_recv.at[d - 1], across).wait_recv()
        c = remote(part, part, gy_send.at[d], gy_recv.at[d], across)
        c.start()
        sends.append(c)
    for k in range(pieces):
        cols = pl.ds(k * wide, wide)
        for d in range(1, nx):
            source = lax.rem(x + nx - d, nx) * 2 + core
            part = ah.at[h_block(source), cols]
            remote(part, part, hx_send.at[k, d - 1], hx_recv.at[k, d - 1], sibling).wait_recv()
            c = remote(part, part, hc_send.at[k, d], hc_recv.at[k, d], sibling)
            c.start()
            sends.append(c)
    for c in own:
        c.wait()
    for c in w_copies:
        c.wait()
    for k in range(pieces):
        cols = pl.ds(k * wide, wide)
        for d in range(nx):
            source = lax.rem(x + nx - d, nx) * 2 + 1 - core
            part = ah.at[h_block(source), cols]
            remote(part, part, hc_send.at[k, d], hc_recv.at[k, d], sibling).wait_recv()
    for d in range(nz):
        source = lax.rem(z + nz - d, nz) * 2 + 1 - y
        part = ag.at[g_block(source)]
        remote(part, part, gy_send.at[d], gy_recv.at[d], across).wait_recv()

    outs = [
        pltpu.make_async_copy(ah, all_hidden_out, out_sem.at[0]),
        pltpu.make_async_copy(ag, all_grad_out, out_sem.at[1]),
    ]
    for c in outs:
        c.start()

    def y_copy(t):
        return remote(p_part.at[t, 1 - y], p_recv.at[t], py_send.at[t], py_recv.at[t], across)

    def z_copy(t, d):
        return remote(
            p_part.at[t, y, lax.rem(z + d, nz)], p_recv_z.at[t, d - 1], pz_send.at[t, d - 1], pz_recv.at[t, d - 1], z_peer(d)
        )

    def c_copy(t):
        return remote(h_part.at[t, 1 - core], h_recv.at[t], qc_send.at[t], qc_recv.at[t], sibling)

    def x_copy(t, d):
        return remote(
            h_part.at[t, core, lax.rem(x + d, nx)], h_recv_x.at[t, d - 1], qx_send.at[t, d - 1], qx_recv.at[t, d - 1], x_peer(d)
        )

    def p_second(t):
        y_copy(t).wait_recv()
        p_part[t, y] += p_recv[t]
        for d in range(1, nz):
            z_copy(t, d).start()

    def h_second(t):
        c_copy(t).wait_recv()
        h_part[t, core] += h_recv[t]
        for d in range(1, nx):
            x_copy(t, d).start()

    @pl.loop(0, nh)
    def _(t):
        @pl.when(t < np_)
        def _():
            cols = pl.ds(pl.multiple_of(t * tp, tp), tp)
            value = jnp.dot(ah[...], w[:, cols], preferred_element_type=jnp.float32)
            for r in range(nrow):
                p_part[t, r % 2, r // 2] = value[r * gb : (r + 1) * gb]
            y_copy(t).start()

        rows = pl.ds(pl.multiple_of(t * th, th), th)
        value = lax.dot_general(ag[...], w[rows, :], (((1,), (1,)), ((), ())), preferred_element_type=jnp.float32)
        for c in range(ncol):
            h_part[t, c % 2, c // 2] = value[c * hb : (c + 1) * hb]
        c_copy(t).start()

        @pl.when(t >= 1)
        def _():
            h_second(t - 1)

    h_second(nh - 1)

    @pl.loop(0, np_)
    def _(t):
        p_second(t)

    @pl.loop(0, nh)
    def _(t):
        total = h_part[t, core, x]
        for d in range(1, nx):
            x_copy(t, d).wait_recv()
            total += h_recv_x[t, d - 1]
        hgrad_out[:, pl.ds(pl.multiple_of(t * th, th), th)] = total.astype(hgrad_out.dtype)

    @pl.loop(0, np_)
    def _(t):
        total = p_part[t, y, z]
        for d in range(1, nz):
            z_copy(t, d).wait_recv()
            total += p_recv_z[t, d - 1]
        proj_out[:, pl.ds(pl.multiple_of(t * tp, tp), tp)] = total.astype(proj_out.dtype)

    for c in sends:
        c.wait_send()
    for c in outs:
        c.wait()

    @pl.loop(0, np_)
    def _(t):
        y_copy(t).wait_send()
        for d in range(1, nz):
            z_copy(t, d).wait_send()

    @pl.loop(0, nh)
    def _(t):
        c_copy(t).wait_send()
        for d in range(1, nx):
            x_copy(t, d).wait_send()


def exchange(nrow, ncol, hidden, weight, grad):
    nz, nx = nrow // 2, ncol // 2
    hb, ff = hidden.shape
    gb, dd = grad.shape
    tp, th = tile_of(dd, 512), tile_of(ff, 512)
    np_, nh = dd // tp, ff // th
    np_ = min(np_, nh)
    tp = dd // np_
    pieces = 2 if ff % 256 == 0 else 1
    f32, bf16 = jnp.float32, jnp.bfloat16
    dma = pltpu.SemaphoreType.DMA
    any_spec = pl.BlockSpec(memory_space=pl.ANY)
    vmem_spec = pl.BlockSpec(memory_space=pltpu.VMEM)
    return pl.pallas_call(
        functools.partial(exchange_kernel, nrow, ncol),
        out_shape=(
            jax.ShapeDtypeStruct((gb, dd), bf16),
            jax.ShapeDtypeStruct((hb, ff), bf16),
            jax.ShapeDtypeStruct((hb * ncol, ff), bf16),
            jax.ShapeDtypeStruct((gb * nrow, dd), bf16),
        ),
        in_specs=[any_spec] * 3,
        out_specs=(vmem_spec, vmem_spec, any_spec, any_spec),
        scratch_shapes=[
            pltpu.VMEM((ff, dd), bf16),
            pltpu.VMEM((hb * ncol, ff), bf16),
            pltpu.VMEM((gb * nrow, dd), bf16),
            pltpu.VMEM((np_, 2, nz, gb, tp), f32),
            pltpu.VMEM((np_, nz, gb, tp), f32),
            pltpu.VMEM((np_, nz - 1, gb, tp), f32),
            pltpu.VMEM((nh, 2, nx, hb, th), f32),
            pltpu.VMEM((nh, nx, hb, th), f32),
            pltpu.VMEM((nh, nx - 1, hb, th), f32),
            dma((nh,)),
            dma((2,)),
            dma((2,)),
            dma((pieces, nx - 1)),
            dma((pieces, nx - 1)),
            dma((pieces, nx)),
            dma((pieces, nx)),
            dma((nz - 1,)),
            dma((nz - 1,)),
            dma((nz,)),
            dma((nz,)),
            dma((np_,)),
            dma((np_,)),
            dma((np_, nz - 1)),
            dma((np_, nz - 1)),
            dma((nh,)),
            dma((nh,)),
            dma((nh, nx - 1)),
            dma((nh, nx - 1)),
        ],
        compiler_params=pltpu.CompilerParams(
            collective_id=0, has_side_effects=True, vmem_limit_bytes=48 * 1024 * 1024
        ),
    )(hidden, weight, grad)


def outer_kernel(scale, h, g, out):
    value = lax.dot_general(h[...], g[...], (((0,), (0,)), ((), ())), preferred_element_type=jnp.float32)
    out[...] = value * scale


def outer(all_hidden, all_grad):
    tokens, ff = all_hidden.shape
    dd = all_grad.shape[1]
    th = tile_of(ff, 512)
    return pl.pallas_call(
        functools.partial(outer_kernel, tokens**-0.5),
        grid=(ff // th,),
        out_shape=jax.ShapeDtypeStruct((ff, dd), jnp.float32),
        in_specs=[pl.BlockSpec((tokens, th), lambda i: (0, i)), pl.BlockSpec((tokens, dd), lambda i: (0, 0))],
        out_specs=pl.BlockSpec((th, dd), lambda i: (i, 0)),
        compiler_params=pltpu.CompilerParams(vmem_limit_bytes=40 * 1024 * 1024),
        cost_estimate=pl.CostEstimate(
            flops=2 * tokens * ff * dd, bytes_accessed=4 * ff * dd + 2 * tokens * (ff + dd), transcendentals=0
        ),
    )(all_hidden, all_grad)


def solution(mesh):
    nrow, ncol = mesh.shape["row"], mesh.shape["col"]

    def on_device(hidden, down_weight, out_grad):
        projected, hidden_grad, all_hidden, all_grad = exchange(nrow, ncol, hidden, down_weight, out_grad)
        return projected, hidden_grad, outer(all_hidden, all_grad)

    return jax.shard_map(
        on_device,
        mesh=mesh,
        in_specs=(P("col", "row"), P("row", "col"), P("row", "col")),
        out_specs=(P("row", "col"), P("col", "row"), P("row", "col")),
        check_vma=False,
    )
```

```python
import functools

import jax
import jax.numpy as jnp
from jax import lax
from jax.experimental import pallas as pl
from jax.experimental.pallas import tpu as pltpu
from jax.sharding import PartitionSpec as P

MESH = pl.DeviceIdType.MESH


def tile_of(extent, most):
    best = 128
    for width in range(128, most + 1, 128):
        if extent % width == 0:
            best = width
    return best


def exchange_kernel(
    nrow,
    ncol,
    hidden,
    weight,
    grad,
    *refs,
):
    nz, nx = nrow // 2, ncol // 2
    p_out, h_out, rest = refs[:nz], refs[nz : nz + nx], refs[nz + nx :]
    exchange_body(nrow, ncol, p_out, h_out, hidden, weight, grad, *rest)


def exchange_body(
    nrow,
    ncol,
    p_out,
    h_out,
    hidden,
    weight,
    grad,
    all_hidden_out,
    all_grad_out,
    w,
    ah,
    ag,
    p_part,
    p_recv,
    h_part,
    h_recv,
    w_sem,
    own_sem,
    out_sem,
    hx_send,
    hx_recv,
    hc_send,
    hc_recv,
    gz_send,
    gz_recv,
    gy_send,
    gy_recv,
    py_send,
    py_recv,
    qc_send,
    qc_recv,
):
    nz, nx = nrow // 2, ncol // 2
    row, col = lax.axis_index("row"), lax.axis_index("col")
    z, y = row // 2, lax.rem(row, 2)
    x, core = col // 2, lax.rem(col, 2)
    sibling = (row, x * 2 + 1 - core)
    across = (z * 2 + 1 - y, col)

    def x_peer(d):
        return (row, lax.rem(x + d, nx) * 2 + core)

    def z_peer(d):
        return (lax.rem(z + d, nz) * 2 + y, col)

    def remote(src, dst, send, recv, device):
        return pltpu.make_async_remote_copy(
            src_ref=src, dst_ref=dst, send_sem=send, recv_sem=recv, device_id=device, device_id_type=MESH
        )

    hb, ff = hidden.shape
    gb, dd = grad.shape
    pieces = hx_recv.shape[0]
    wide = ff // pieces
    np_, tp = p_part.shape[0], p_part.shape[-1]
    nh, th = h_part.shape[0], h_part.shape[-1]

    w_copies = []
    for t in range(nh):
        rows = pl.ds(t * th, th)
        c = pltpu.make_async_copy(weight.at[rows], w.at[rows], w_sem.at[t])
        c.start()
        w_copies.append(c)

    def h_block(owner):
        return pl.ds(pl.multiple_of(owner * hb, hb), hb)

    def g_block(owner):
        return pl.ds(pl.multiple_of(owner * gb, gb), gb)

    own = [
        pltpu.make_async_copy(hidden, ah.at[h_block(col)], own_sem.at[0]),
        pltpu.make_async_copy(grad, ag.at[g_block(row)], own_sem.at[1]),
    ]
    for c in own:
        c.start()

    barrier = pltpu.get_barrier_semaphore()
    peers = [sibling, across] + [x_peer(d) for d in range(1, nx)] + [z_peer(d) for d in range(1, nz)]
    for peer in peers:
        pl.semaphore_signal(barrier, inc=1, device_id=peer, device_id_type=MESH)
    pl.semaphore_wait(barrier, len(peers))

    sends = []
    for k in range(pieces):
        cols = pl.ds(k * wide, wide)
        for d in range(1, nx):
            c = remote(
                hidden.at[:, cols], ah.at[h_block(col), cols], hx_send.at[k, d - 1], hx_recv.at[k, d - 1], x_peer(d)
            )
            c.start()
            sends.append(c)
    for d in range(1, nz):
        c = remote(grad, ag.at[g_block(row)], gz_send.at[d - 1], gz_recv.at[d - 1], z_peer(d))
        c.start()
        sends.append(c)
    c = remote(grad, ag.at[g_block(row)], gy_send.at[0], gy_recv.at[0], across)
    c.start()
    sends.append(c)
    for k in range(pieces):
        cols = pl.ds(k * wide, wide)
        c = remote(hidden.at[:, cols], ah.at[h_block(col), cols], hc_send.at[k, 0], hc_recv.at[k, 0], sibling)
        c.start()
        sends.append(c)

    def forward_grad(d):
        source = lax.rem(z + nz - d, nz) * 2 + y
        part = ag.at[g_block(source)]
        remote(part, part, gz_send.at[d - 1], gz_recv.at[d - 1], across).wait_recv()
        c = remote(part, part, gy_send.at[d], gy_recv.at[d], across)
        c.start()
        sends.append(c)

    def forward_hidden(k, d):
        source = lax.rem(x + nx - d, nx) * 2 + core
        part = ah.at[h_block(source), pl.ds(k * wide, wide)]
        remote(part, part, hx_send.at[k, d - 1], hx_recv.at[k, d - 1], sibling).wait_recv()
        c = remote(part, part, hc_send.at[k, d], hc_recv.at[k, d], sibling)
        c.start()
        sends.append(c)

    from_x = [(k, d) for k in range(pieces) for d in range(1, nx)]
    for step in range(max(nz - 1, len(from_x))):
        if step < nz - 1:
            forward_grad(step + 1)
        if step < len(from_x):
            forward_hidden(*from_x[step])
    for c in own:
        c.wait()
    for c in w_copies:
        c.wait()
    for k in range(pieces):
        cols = pl.ds(k * wide, wide)
        for d in range(nx):
            source = lax.rem(x + nx - d, nx) * 2 + 1 - core
            part = ah.at[h_block(source), cols]
            remote(part, part, hc_send.at[k, d], hc_recv.at[k, d], sibling).wait_recv()

    def y_copy(t):
        return remote(p_part.at[t, 1 - y], p_recv.at[t], py_send.at[t], py_recv.at[t], across)

    def c_copy(t):
        return remote(h_part.at[t, 1 - core], h_recv.at[t], qc_send.at[t], qc_recv.at[t], sibling)

    def p_second(t):
        y_copy(t).wait_recv()
        cols = pl.ds(pl.multiple_of(t * tp, tp), tp)
        for d in range(nz):
            at = lax.rem(z + d, nz)
            p_out[d][:, cols] = p_part[t, y, at] + p_recv[t, at]

    def h_second(t):
        c_copy(t).wait_recv()
        cols = pl.ds(pl.multiple_of(t * th, th), th)
        for d in range(nx):
            at = lax.rem(x + d, nx)
            h_out[d][:, cols] = h_part[t, core, at] + h_recv[t, at]

    @pl.loop(0, np_)
    def _(t):
        cols = pl.ds(pl.multiple_of(t * tp, tp), tp)
        value = jnp.dot(ah[...], w[:, cols], preferred_element_type=jnp.float32)
        for r in range(nrow):
            p_part[t, r % 2, r // 2] = value[r * gb : (r + 1) * gb]
        y_copy(t).start()

    for d in range(nz):
        source = lax.rem(z + nz - d, nz) * 2 + 1 - y
        part = ag.at[g_block(source)]
        remote(part, part, gy_send.at[d], gy_recv.at[d], across).wait_recv()
    outs = [
        pltpu.make_async_copy(ah, all_hidden_out, out_sem.at[0]),
        pltpu.make_async_copy(ag, all_grad_out, out_sem.at[1]),
    ]
    for c in outs:
        c.start()

    @pl.loop(0, nh)
    def _(t):
        rows = pl.ds(pl.multiple_of(t * th, th), th)
        value = lax.dot_general(ag[...], w[rows, :], (((1,), (1,)), ((), ())), preferred_element_type=jnp.float32)
        for c in range(ncol):
            h_part[t, c % 2, c // 2] = value[c * hb : (c + 1) * hb]
        c_copy(t).start()

        @pl.when(t >= 1)
        def _():
            h_second(t - 1)

    h_second(nh - 1)

    @pl.loop(0, np_)
    def _(t):
        p_second(t)

    for c in sends:
        c.wait_send()
    for c in outs:
        c.wait()

    @pl.loop(0, np_)
    def _(t):
        y_copy(t).wait_send()

    @pl.loop(0, nh)
    def _(t):
        c_copy(t).wait_send()


def exchange(nrow, ncol, hidden, weight, grad):
    nz, nx = nrow // 2, ncol // 2
    hb, ff = hidden.shape
    gb, dd = grad.shape
    tp, th = tile_of(dd, 512), tile_of(ff, 512)
    np_, nh = dd // tp, ff // th
    np_ = min(np_, nh)
    tp = dd // np_
    pieces = 2 if ff % 256 == 0 else 1
    f32, bf16 = jnp.float32, jnp.bfloat16
    dma = pltpu.SemaphoreType.DMA
    any_spec = pl.BlockSpec(memory_space=pl.ANY)
    vmem_spec = pl.BlockSpec(memory_space=pltpu.VMEM)
    return pl.pallas_call(
        functools.partial(exchange_kernel, nrow, ncol),
        out_shape=(
            *[jax.ShapeDtypeStruct((gb, dd), f32)] * nz,
            *[jax.ShapeDtypeStruct((hb, ff), f32)] * nx,
            jax.ShapeDtypeStruct((hb * ncol, ff), bf16),
            jax.ShapeDtypeStruct((gb * nrow, dd), bf16),
        ),
        in_specs=[any_spec] * 3,
        out_specs=(*[vmem_spec] * (nz + nx), any_spec, any_spec),
        scratch_shapes=[
            pltpu.VMEM((ff, dd), bf16),
            pltpu.VMEM((hb * ncol, ff), bf16),
            pltpu.VMEM((gb * nrow, dd), bf16),
            pltpu.VMEM((np_, 2, nz, gb, tp), f32),
            pltpu.VMEM((np_, nz, gb, tp), f32),
            pltpu.VMEM((nh, 2, nx, hb, th), f32),
            pltpu.VMEM((nh, nx, hb, th), f32),
            dma((nh,)),
            dma((2,)),
            dma((2,)),
            dma((pieces, nx - 1)),
            dma((pieces, nx - 1)),
            dma((pieces, nx)),
            dma((pieces, nx)),
            dma((nz - 1,)),
            dma((nz - 1,)),
            dma((nz,)),
            dma((nz,)),
            dma((np_,)),
            dma((np_,)),
            dma((nh,)),
            dma((nh,)),
        ],
        compiler_params=pltpu.CompilerParams(
            collective_id=0, has_side_effects=True, vmem_limit_bytes=48 * 1024 * 1024
        ),
    )(hidden, weight, grad)


def outer_kernel(scale, h, g, out):
    value = lax.dot_general(h[...], g[...], (((0,), (0,)), ((), ())), preferred_element_type=jnp.float32)
    out[...] = value * scale


def outer(all_hidden, all_grad):
    tokens, ff = all_hidden.shape
    dd = all_grad.shape[1]
    th = tile_of(ff, 512)
    return pl.pallas_call(
        functools.partial(outer_kernel, tokens**-0.5),
        grid=(ff // th,),
        out_shape=jax.ShapeDtypeStruct((ff, dd), jnp.float32),
        in_specs=[pl.BlockSpec((tokens, th), lambda i: (0, i)), pl.BlockSpec((tokens, dd), lambda i: (0, 0))],
        out_specs=pl.BlockSpec((th, dd), lambda i: (i, 0)),
        compiler_params=pltpu.CompilerParams(vmem_limit_bytes=40 * 1024 * 1024),
        cost_estimate=pl.CostEstimate(
            flops=2 * tokens * ff * dd, bytes_accessed=4 * ff * dd + 2 * tokens * (ff + dd), transcendentals=0
        ),
    )(all_hidden, all_grad)


def solution(mesh):
    nrow, ncol = mesh.shape["row"], mesh.shape["col"]

    nz, nx = nrow // 2, ncol // 2

    def shifted(value, axis, groups, d):
        pairs = [(g * 2 + o, (g + d) % groups * 2 + o) for g in range(groups) for o in range(2)]
        return lax.ppermute(value, axis, pairs)

    def on_device(hidden, down_weight, out_grad):
        *sums, all_hidden, all_grad = exchange(nrow, ncol, hidden, down_weight, out_grad)
        p_sums, h_sums = sums[:nz], sums[nz:]
        h_total = h_sums[0]
        for d in range(1, nx):
            h_total += shifted(h_sums[d], "col", nx, d)
        p_total = p_sums[0]
        for d in range(1, nz):
            p_total += shifted(p_sums[d], "row", nz, d)
        weight_grad = outer(all_hidden, all_grad)
        return p_total.astype(jnp.bfloat16), h_total.astype(jnp.bfloat16), weight_grad

    return jax.shard_map(
        on_device,
        mesh=mesh,
        in_specs=(P("col", "row"), P("row", "col"), P("row", "col")),
        out_specs=(P("row", "col"), P("col", "row"), P("row", "col")),
        check_vma=False,
    )
```

```python
import functools

import jax
import jax.numpy as jnp
from jax import lax
from jax.experimental import pallas as pl
from jax.experimental.pallas import tpu as pltpu
from jax.sharding import PartitionSpec as P

MESH = pl.DeviceIdType.MESH


def tile_of(extent, most):
    best = 128
    for width in range(128, most + 1, 128):
        if extent % width == 0:
            best = width
    return best


def exchange_kernel(
    nrow,
    ncol,
    early,
    hidden,
    weight,
    grad,
    *refs,
):
    nz, nx = nrow // 2, ncol // 2
    outputs = nz + early
    p_out, h_out, rest = refs[:outputs], refs[outputs : outputs + nx], refs[outputs + nx :]
    exchange_body(nrow, ncol, early, p_out, h_out, hidden, weight, grad, *rest)


def exchange_body(
    nrow,
    ncol,
    nf,
    p_out,
    h_out,
    hidden,
    weight,
    grad,
    all_hidden_out,
    all_grad_out,
    w,
    ah,
    ag,
    p_part,
    p_recv,
    z_recv,
    y_last,
    h_part,
    h_recv,
    w_sem,
    own_sem,
    out_sem,
    hx_send,
    hx_recv,
    hc_send,
    hc_recv,
    gz_send,
    gz_recv,
    gy_send,
    gy_recv,
    py_send,
    py_recv,
    pz_send,
    pz_recv,
    pl_send,
    pl_recv,
    qc_send,
    qc_recv,
):
    nz, nx = nrow // 2, ncol // 2
    row, col = lax.axis_index("row"), lax.axis_index("col")
    z, y = row // 2, lax.rem(row, 2)
    x, core = col // 2, lax.rem(col, 2)
    sibling = (row, x * 2 + 1 - core)
    across = (z * 2 + 1 - y, col)

    def x_peer(d):
        return (row, lax.rem(x + d, nx) * 2 + core)

    def z_peer(d):
        return (lax.rem(z + d, nz) * 2 + y, col)

    def remote(src, dst, send, recv, device):
        return pltpu.make_async_remote_copy(
            src_ref=src, dst_ref=dst, send_sem=send, recv_sem=recv, device_id=device, device_id_type=MESH
        )

    hb, ff = hidden.shape
    gb, dd = grad.shape
    pieces = hx_recv.shape[0]
    wide = ff // pieces
    np_, tp = p_part.shape[0], p_part.shape[-1]
    nh, th = h_part.shape[0], h_part.shape[-1]

    w_copies = []
    for t in range(nh):
        rows = pl.ds(t * th, th)
        c = pltpu.make_async_copy(weight.at[rows], w.at[rows], w_sem.at[t])
        c.start()
        w_copies.append(c)

    def h_block(owner):
        return pl.ds(pl.multiple_of(owner * hb, hb), hb)

    def g_block(owner):
        return pl.ds(pl.multiple_of(owner * gb, gb), gb)

    own = [
        pltpu.make_async_copy(hidden, ah.at[h_block(col)], own_sem.at[0]),
        pltpu.make_async_copy(grad, ag.at[g_block(row)], own_sem.at[1]),
    ]
    for c in own:
        c.start()

    barrier = pltpu.get_barrier_semaphore()
    peers = [sibling, across] + [x_peer(d) for d in range(1, nx)] + [z_peer(d) for d in range(1, nz)]
    for peer in peers:
        pl.semaphore_signal(barrier, inc=1, device_id=peer, device_id_type=MESH)
    pl.semaphore_wait(barrier, len(peers))

    sends = []
    for k in range(pieces):
        cols = pl.ds(k * wide, wide)
        for d in range(1, nx):
            c = remote(
                hidden.at[:, cols], ah.at[h_block(col), cols], hx_send.at[k, d - 1], hx_recv.at[k, d - 1], x_peer(d)
            )
            c.start()
            sends.append(c)
    for d in range(1, nz):
        c = remote(grad, ag.at[g_block(row)], gz_send.at[d - 1], gz_recv.at[d - 1], z_peer(d))
        c.start()
        sends.append(c)
    c = remote(grad, ag.at[g_block(row)], gy_send.at[0], gy_recv.at[0], across)
    c.start()
    sends.append(c)
    for k in range(pieces):
        cols = pl.ds(k * wide, wide)
        c = remote(hidden.at[:, cols], ah.at[h_block(col), cols], hc_send.at[k, 0], hc_recv.at[k, 0], sibling)
        c.start()
        sends.append(c)

    def forward_grad(d):
        source = lax.rem(z + nz - d, nz) * 2 + y
        part = ag.at[g_block(source)]
        remote(part, part, gz_send.at[d - 1], gz_recv.at[d - 1], across).wait_recv()
        c = remote(part, part, gy_send.at[d], gy_recv.at[d], across)
        c.start()
        sends.append(c)

    def forward_hidden(k, d):
        source = lax.rem(x + nx - d, nx) * 2 + core
        part = ah.at[h_block(source), pl.ds(k * wide, wide)]
        remote(part, part, hx_send.at[k, d - 1], hx_recv.at[k, d - 1], sibling).wait_recv()
        c = remote(part, part, hc_send.at[k, d], hc_recv.at[k, d], sibling)
        c.start()
        sends.append(c)

    from_x = [(k, d) for k in range(pieces) for d in range(1, nx)]
    for step in range(max(nz - 1, len(from_x))):
        if step < nz - 1:
            forward_grad(step + 1)
        if step < len(from_x):
            forward_hidden(*from_x[step])
    for c in own:
        c.wait()
    for c in w_copies:
        c.wait()

    def arrived(k):
        for d in range(nx):
            source = lax.rem(x + nx - d, nx) * 2 + 1 - core
            part = ah.at[h_block(source), pl.ds(k * wide, wide)]
            remote(part, part, hc_send.at[k, d], hc_recv.at[k, d], sibling).wait_recv()

    def y_copy(t):
        return remote(p_part.at[t, 1 - y], p_recv.at[t], py_send.at[t], py_recv.at[t], across)

    def z_copy(d):
        return remote(
            p_part.at[0, :, lax.rem(z + d, nz)], z_recv.at[d - 1], pz_send.at[d - 1], pz_recv.at[d - 1], z_peer(d)
        )

    def last_copy():
        return remote(p_part.at[0, 1 - y, z], y_last, pl_send.at[0], pl_recv.at[0], across)

    def z_sum():
        for d in range(1, nz):
            z_copy(d).wait_recv()
        for half in range(2):
            total = p_part[0, half, z]
            for d in range(1, nz):
                total += z_recv[d - 1, half]
            p_part[0, half, z] = total
        last_copy().start()

    def c_copy(t):
        return remote(h_part.at[t, 1 - core], h_recv.at[t], qc_send.at[t], qc_recv.at[t], sibling)

    def p_second(t):
        y_copy(t).wait_recv()
        cols = pl.ds(pl.multiple_of((t - nf) * tp, tp), tp)
        for d in range(nz):
            at = lax.rem(z + d, nz)
            p_out[d][:, cols] = p_part[t, y, at] + p_recv[t, at]

    def h_second(t):
        c_copy(t).wait_recv()
        cols = pl.ds(pl.multiple_of(t * th, th), th)
        for d in range(nx):
            at = lax.rem(x + d, nx)
            h_out[d][:, cols] = h_part[t, core, at] + h_recv[t, at]

    for k in range(pieces):
        arrived(k)

    @pl.loop(0, np_)
    def _(t):
        cols = pl.ds(pl.multiple_of(t * tp, tp), tp)
        value = jnp.dot(ah[...], w[:, cols], preferred_element_type=jnp.float32)
        for r in range(nrow):
            p_part[t, r % 2, r // 2] = value[r * gb : (r + 1) * gb]

        @pl.when(t >= nf)
        def _():
            y_copy(t).start()

        @pl.when(t < nf)
        def _():
            for d in range(1, nz):
                z_copy(d).start()

    for d in range(nz):
        source = lax.rem(z + nz - d, nz) * 2 + 1 - y
        part = ag.at[g_block(source)]
        remote(part, part, gy_send.at[d], gy_recv.at[d], across).wait_recv()
    outs = [
        pltpu.make_async_copy(ah, all_hidden_out, out_sem.at[0]),
        pltpu.make_async_copy(ag, all_grad_out, out_sem.at[1]),
    ]
    for c in outs:
        c.start()

    @pl.loop(0, nh)
    def _(t):
        rows = pl.ds(pl.multiple_of(t * th, th), th)
        value = lax.dot_general(ag[...], w[rows, :], (((1,), (1,)), ((), ())), preferred_element_type=jnp.float32)
        for c in range(ncol):
            h_part[t, c % 2, c // 2] = value[c * hb : (c + 1) * hb]
        c_copy(t).start()

        @pl.when(t >= 1)
        def _():
            h_second(t - 1)

    if nf:
        z_sum()
    h_second(nh - 1)

    @pl.loop(nf, np_)
    def _(t):
        p_second(t)

    if nf:
        last_copy().wait_recv()
        p_out[nz][...] = p_part[0, y, z] + y_last[...]
        last_copy().wait_send()
        for d in range(1, nz):
            z_copy(d).wait_send()

    for c in sends:
        c.wait_send()
    for c in outs:
        c.wait()

    @pl.loop(nf, np_)
    def _(t):
        y_copy(t).wait_send()

    @pl.loop(0, nh)
    def _(t):
        c_copy(t).wait_send()


def exchange(nrow, ncol, hidden, weight, grad):
    nz, nx = nrow // 2, ncol // 2
    hb, ff = hidden.shape
    gb, dd = grad.shape
    tp, th = tile_of(dd, 512), tile_of(ff, 512)
    np_, nh = dd // tp, ff // th
    np_ = min(np_, nh)
    tp = dd // np_
    early = 1 if np_ > 2 else 0
    kept = [jax.ShapeDtypeStruct((gb, tp), jnp.float32)] * early
    pieces = 2 if ff % 256 == 0 else 1
    f32, bf16 = jnp.float32, jnp.bfloat16
    dma = pltpu.SemaphoreType.DMA
    any_spec = pl.BlockSpec(memory_space=pl.ANY)
    vmem_spec = pl.BlockSpec(memory_space=pltpu.VMEM)
    return pl.pallas_call(
        functools.partial(exchange_kernel, nrow, ncol, early),
        out_shape=(
            *[jax.ShapeDtypeStruct((gb, dd - early * tp), f32)] * nz,
            *kept,
            *[jax.ShapeDtypeStruct((hb, ff), f32)] * nx,
            jax.ShapeDtypeStruct((hb * ncol, ff), bf16),
            jax.ShapeDtypeStruct((gb * nrow, dd), bf16),
        ),
        in_specs=[any_spec] * 3,
        out_specs=(*[vmem_spec] * (nz + early + nx), any_spec, any_spec),
        scratch_shapes=[
            pltpu.VMEM((ff, dd), bf16),
            pltpu.VMEM((hb * ncol, ff), bf16),
            pltpu.VMEM((gb * nrow, dd), bf16),
            pltpu.VMEM((np_, 2, nz, gb, tp), f32),
            pltpu.VMEM((np_, nz, gb, tp), f32),
            pltpu.VMEM((nz - 1, 2, gb, tp), f32),
            pltpu.VMEM((gb, tp), f32),
            pltpu.VMEM((nh, 2, nx, hb, th), f32),
            pltpu.VMEM((nh, nx, hb, th), f32),
            dma((nh,)),
            dma((2,)),
            dma((2,)),
            dma((pieces, nx - 1)),
            dma((pieces, nx - 1)),
            dma((pieces, nx)),
            dma((pieces, nx)),
            dma((nz - 1,)),
            dma((nz - 1,)),
            dma((nz,)),
            dma((nz,)),
            dma((np_,)),
            dma((np_,)),
            dma((nz - 1,)),
            dma((nz - 1,)),
            dma((1,)),
            dma((1,)),
            dma((nh,)),
            dma((nh,)),
        ],
        compiler_params=pltpu.CompilerParams(
            collective_id=0, has_side_effects=True, vmem_limit_bytes=48 * 1024 * 1024
        ),
    )(hidden, weight, grad)


def outer_kernel(scale, h, g, out):
    value = lax.dot_general(h[...], g[...], (((0,), (0,)), ((), ())), preferred_element_type=jnp.float32)
    out[...] = value * scale


def outer(all_hidden, all_grad):
    tokens, ff = all_hidden.shape
    dd = all_grad.shape[1]
    th = tile_of(ff, 512)
    return pl.pallas_call(
        functools.partial(outer_kernel, tokens**-0.5),
        grid=(ff // th,),
        out_shape=jax.ShapeDtypeStruct((ff, dd), jnp.float32),
        in_specs=[pl.BlockSpec((tokens, th), lambda i: (0, i)), pl.BlockSpec((tokens, dd), lambda i: (0, 0))],
        out_specs=pl.BlockSpec((th, dd), lambda i: (i, 0)),
        compiler_params=pltpu.CompilerParams(vmem_limit_bytes=40 * 1024 * 1024),
        cost_estimate=pl.CostEstimate(
            flops=2 * tokens * ff * dd, bytes_accessed=4 * ff * dd + 2 * tokens * (ff + dd), transcendentals=0
        ),
    )(all_hidden, all_grad)


def solution(mesh):
    nrow, ncol = mesh.shape["row"], mesh.shape["col"]

    nz, nx = nrow // 2, ncol // 2

    def shifted(value, axis, groups, d):
        pairs = [(g * 2 + o, (g + d) % groups * 2 + o) for g in range(groups) for o in range(2)]
        return lax.ppermute(value, axis, pairs)

    def on_device(hidden, down_weight, out_grad):
        *sums, all_hidden, all_grad = exchange(nrow, ncol, hidden, down_weight, out_grad)
        p_sums, early, h_sums = sums[:nz], sums[nz:-nx], sums[-nx:]
        h_total = h_sums[0]
        for d in range(1, nx):
            h_total += shifted(h_sums[d], "col", nx, d)
        p_total = p_sums[0]
        for d in range(1, nz):
            p_total += shifted(p_sums[d], "row", nz, d)
        p_total = jnp.concatenate([*early, p_total], axis=1)
        weight_grad = outer(all_hidden, all_grad)
        return p_total.astype(jnp.bfloat16), h_total.astype(jnp.bfloat16), weight_grad

    return jax.shard_map(
        on_device,
        mesh=mesh,
        in_specs=(P("col", "row"), P("row", "col"), P("row", "col")),
        out_specs=(P("row", "col"), P("col", "row"), P("row", "col")),
        check_vma=False,
    )
```

```python
import functools

import jax
import jax.numpy as jnp
from jax import lax
from jax.experimental import pallas as pl
from jax.experimental.pallas import tpu as pltpu
from jax.sharding import PartitionSpec as P

MESH = pl.DeviceIdType.MESH


def tile_of(extent, most):
    best = 128
    for width in range(128, most + 1, 128):
        if extent % width == 0:
            best = width
    return best


def exchange_kernel(
    nrow,
    ncol,
    early,
    hidden,
    weight,
    grad,
    *refs,
):
    nz, nx = nrow // 2, ncol // 2
    outputs = nz + early
    p_out, h_out, rest = refs[:outputs], refs[outputs : outputs + nx], refs[outputs + nx :]
    exchange_body(nrow, ncol, early, p_out, h_out, hidden, weight, grad, *rest)


def exchange_body(
    nrow,
    ncol,
    nf,
    p_out,
    h_out,
    hidden,
    weight,
    grad,
    all_hidden_out,
    all_grad_out,
    w,
    ah,
    ag,
    p_part,
    p_recv,
    z_recv,
    y_last,
    h_part,
    h_recv,
    w_sem,
    own_sem,
    out_sem,
    hx_send,
    hx_recv,
    hc_send,
    hc_recv,
    gz_send,
    gz_recv,
    gy_send,
    gy_recv,
    py_send,
    py_recv,
    pz_send,
    pz_recv,
    pl_send,
    pl_recv,
    qc_send,
    qc_recv,
):
    nz, nx = nrow // 2, ncol // 2
    row, col = lax.axis_index("row"), lax.axis_index("col")
    z, y = row // 2, lax.rem(row, 2)
    x, core = col // 2, lax.rem(col, 2)
    sibling = (row, x * 2 + 1 - core)
    across = (z * 2 + 1 - y, col)

    def x_peer(d):
        return (row, lax.rem(x + d, nx) * 2 + core)

    def z_peer(d):
        return (lax.rem(z + d, nz) * 2 + y, col)

    def remote(src, dst, send, recv, device):
        return pltpu.make_async_remote_copy(
            src_ref=src, dst_ref=dst, send_sem=send, recv_sem=recv, device_id=device, device_id_type=MESH
        )

    hb, ff = hidden.shape
    gb, dd = grad.shape
    pieces = hx_recv.shape[0]
    wide = ff // pieces
    np_, tp = p_part.shape[0], p_part.shape[-1]
    nh, th = h_part.shape[0], h_part.shape[-1]

    w_copies = []
    for t in range(nh):
        rows = pl.ds(t * th, th)
        c = pltpu.make_async_copy(weight.at[rows], w.at[rows], w_sem.at[t])
        c.start()
        w_copies.append(c)

    def h_block(owner):
        return pl.ds(pl.multiple_of(owner * hb, hb), hb)

    def g_block(owner):
        return pl.ds(pl.multiple_of(owner * gb, gb), gb)

    own = [
        pltpu.make_async_copy(hidden, ah.at[h_block(col)], own_sem.at[0]),
        pltpu.make_async_copy(grad, ag.at[g_block(row)], own_sem.at[1]),
    ]
    for c in own:
        c.start()

    barrier = pltpu.get_barrier_semaphore()
    peers = [sibling, across] + [x_peer(d) for d in range(1, nx)] + [z_peer(d) for d in range(1, nz)]
    for peer in peers:
        pl.semaphore_signal(barrier, inc=1, device_id=peer, device_id_type=MESH)
    pl.semaphore_wait(barrier, len(peers))

    sends = []
    for k in range(pieces):
        cols = pl.ds(k * wide, wide)
        for d in range(1, nx):
            c = remote(
                hidden.at[:, cols], ah.at[h_block(col), cols], hx_send.at[k, d - 1], hx_recv.at[k, d - 1], x_peer(d)
            )
            c.start()
            sends.append(c)
    for d in range(1, nz):
        c = remote(grad, ag.at[g_block(row)], gz_send.at[d - 1], gz_recv.at[d - 1], z_peer(d))
        c.start()
        sends.append(c)
    c = remote(grad, ag.at[g_block(row)], gy_send.at[0], gy_recv.at[0], across)
    c.start()
    sends.append(c)
    for k in range(pieces):
        cols = pl.ds(k * wide, wide)
        c = remote(hidden.at[:, cols], ah.at[h_block(col), cols], hc_send.at[k, 0], hc_recv.at[k, 0], sibling)
        c.start()
        sends.append(c)

    def forward_grad(d):
        source = lax.rem(z + nz - d, nz) * 2 + y
        part = ag.at[g_block(source)]
        remote(part, part, gz_send.at[d - 1], gz_recv.at[d - 1], across).wait_recv()
        c = remote(part, part, gy_send.at[d], gy_recv.at[d], across)
        c.start()
        sends.append(c)

    def forward_hidden(k, d):
        source = lax.rem(x + nx - d, nx) * 2 + core
        part = ah.at[h_block(source), pl.ds(k * wide, wide)]
        remote(part, part, hx_send.at[k, d - 1], hx_recv.at[k, d - 1], sibling).wait_recv()
        c = remote(part, part, hc_send.at[k, d], hc_recv.at[k, d], sibling)
        c.start()
        sends.append(c)

    from_x = [(k, d) for k in range(pieces) for d in range(1, nx)]
    for step in range(max(nz - 1, len(from_x))):
        if step < nz - 1:
            forward_grad(step + 1)
        if step < len(from_x):
            forward_hidden(*from_x[step])
    for c in own:
        c.wait()
    for c in w_copies:
        c.wait()

    def arrived(k):
        for d in range(nx):
            source = lax.rem(x + nx - d, nx) * 2 + 1 - core
            part = ah.at[h_block(source), pl.ds(k * wide, wide)]
            remote(part, part, hc_send.at[k, d], hc_recv.at[k, d], sibling).wait_recv()

    def y_copy(t):
        return remote(p_part.at[t, 1 - y], p_recv.at[t], py_send.at[t], py_recv.at[t], across)

    def z_copy(d):
        return remote(
            p_part.at[0, :, lax.rem(z + d, nz)], z_recv.at[d - 1], pz_send.at[d - 1], pz_recv.at[d - 1], z_peer(d)
        )

    def last_copy():
        return remote(p_part.at[0, 1 - y, z], y_last, pl_send.at[0], pl_recv.at[0], across)

    def z_sum():
        for d in range(1, nz):
            z_copy(d).wait_recv()
        for half in range(2):
            total = p_part[0, half, z]
            for d in range(1, nz):
                total += z_recv[d - 1, half]
            p_part[0, half, z] = total
        last_copy().start()

    def c_copy(t):
        return remote(h_part.at[t, 1 - core], h_recv.at[t], qc_send.at[t], qc_recv.at[t], sibling)

    def p_second(t):
        y_copy(t).wait_recv()
        cols = pl.ds(pl.multiple_of((t - nf) * tp, tp), tp)
        for d in range(nz):
            at = lax.rem(z + d, nz)
            p_out[d][:, cols] = p_part[t, y, at] + p_recv[t, at]

    def h_second(t):
        c_copy(t).wait_recv()
        cols = pl.ds(pl.multiple_of(t * th, th), th)
        for d in range(nx):
            at = lax.rem(x + d, nx)
            h_out[d][:, cols] = h_part[t, core, at] + h_recv[t, at]

    for k in range(pieces):
        arrived(k)

    @pl.loop(0, np_)
    def _(t):
        cols = pl.ds(pl.multiple_of(t * tp, tp), tp)
        value = jnp.dot(ah[...], w[:, cols], preferred_element_type=jnp.float32)
        for r in range(nrow):
            p_part[t, r % 2, r // 2] = value[r * gb : (r + 1) * gb]

        @pl.when(t >= nf)
        def _():
            y_copy(t).start()

        @pl.when(t < nf)
        def _():
            for d in range(1, nz):
                z_copy(d).start()

    for d in range(nz):
        source = lax.rem(z + nz - d, nz) * 2 + 1 - y
        part = ag.at[g_block(source)]
        remote(part, part, gy_send.at[d], gy_recv.at[d], across).wait_recv()
    outs = [
        pltpu.make_async_copy(ah, all_hidden_out, out_sem.at[0]),
        pltpu.make_async_copy(ag, all_grad_out, out_sem.at[1]),
    ]
    for c in outs:
        c.start()

    @pl.loop(0, nh)
    def _(t):
        rows = pl.ds(pl.multiple_of(t * th, th), th)
        value = lax.dot_general(ag[...], w[rows, :], (((1,), (1,)), ((), ())), preferred_element_type=jnp.float32)
        for c in range(ncol):
            h_part[t, c % 2, c // 2] = value[c * hb : (c + 1) * hb]
        c_copy(t).start()

        @pl.when(t >= 1)
        def _():
            h_second(t - 1)

    if nf:
        z_sum()
    h_second(nh - 1)

    @pl.loop(nf, np_)
    def _(t):
        p_second(t)

    if nf:
        last_copy().wait_recv()
        p_out[nz][...] = p_part[0, y, z] + y_last[...]
        last_copy().wait_send()
        for d in range(1, nz):
            z_copy(d).wait_send()

    for c in sends:
        c.wait_send()
    for c in outs:
        c.wait()

    @pl.loop(nf, np_)
    def _(t):
        y_copy(t).wait_send()

    @pl.loop(0, nh)
    def _(t):
        c_copy(t).wait_send()


def exchange(nrow, ncol, hidden, weight, grad):
    nz, nx = nrow // 2, ncol // 2
    hb, ff = hidden.shape
    gb, dd = grad.shape
    tp, th = tile_of(dd, 512), tile_of(ff, 512)
    np_, nh = dd // tp, ff // th
    np_ = min(np_, nh)
    tp = dd // np_
    early = 1 if np_ > 2 else 0
    kept = [jax.ShapeDtypeStruct((gb, tp), jnp.float32)] * early
    pieces = 2 if ff % 256 == 0 else 1
    f32, bf16 = jnp.float32, jnp.bfloat16
    dma = pltpu.SemaphoreType.DMA
    any_spec = pl.BlockSpec(memory_space=pl.ANY)
    vmem_spec = pl.BlockSpec(memory_space=pltpu.VMEM)
    return pl.pallas_call(
        functools.partial(exchange_kernel, nrow, ncol, early),
        out_shape=(
            *[jax.ShapeDtypeStruct((gb, dd - early * tp), f32)] * nz,
            *kept,
            *[jax.ShapeDtypeStruct((hb, ff), f32)] * nx,
            jax.ShapeDtypeStruct((hb * ncol, ff), bf16),
            jax.ShapeDtypeStruct((gb * nrow, dd), bf16),
        ),
        in_specs=[vmem_spec, any_spec, vmem_spec],
        out_specs=(*[vmem_spec] * (nz + early + nx), any_spec, any_spec),
        scratch_shapes=[
            pltpu.VMEM((ff, dd), bf16),
            pltpu.VMEM((hb * ncol, ff), bf16),
            pltpu.VMEM((gb * nrow, dd), bf16),
            pltpu.VMEM((np_, 2, nz, gb, tp), f32),
            pltpu.VMEM((np_, nz, gb, tp), f32),
            pltpu.VMEM((nz - 1, 2, gb, tp), f32),
            pltpu.VMEM((gb, tp), f32),
            pltpu.VMEM((nh, 2, nx, hb, th), f32),
            pltpu.VMEM((nh, nx, hb, th), f32),
            dma((nh,)),
            dma((2,)),
            dma((2,)),
            dma((pieces, nx - 1)),
            dma((pieces, nx - 1)),
            dma((pieces, nx)),
            dma((pieces, nx)),
            dma((nz - 1,)),
            dma((nz - 1,)),
            dma((nz,)),
            dma((nz,)),
            dma((np_,)),
            dma((np_,)),
            dma((nz - 1,)),
            dma((nz - 1,)),
            dma((1,)),
            dma((1,)),
            dma((nh,)),
            dma((nh,)),
        ],
        compiler_params=pltpu.CompilerParams(
            collective_id=0, has_side_effects=True, vmem_limit_bytes=48 * 1024 * 1024
        ),
    )(hidden, weight, grad)


def outer_kernel(scale, h, g, out):
    value = lax.dot_general(h[...], g[...], (((0,), (0,)), ((), ())), preferred_element_type=jnp.float32)
    out[...] = value * scale


def outer(all_hidden, all_grad):
    tokens, ff = all_hidden.shape
    dd = all_grad.shape[1]
    th = tile_of(ff, 512)
    return pl.pallas_call(
        functools.partial(outer_kernel, tokens**-0.5),
        grid=(ff // th,),
        out_shape=jax.ShapeDtypeStruct((ff, dd), jnp.float32),
        in_specs=[pl.BlockSpec((tokens, th), lambda i: (0, i)), pl.BlockSpec((tokens, dd), lambda i: (0, 0))],
        out_specs=pl.BlockSpec((th, dd), lambda i: (i, 0)),
        compiler_params=pltpu.CompilerParams(vmem_limit_bytes=40 * 1024 * 1024),
        cost_estimate=pl.CostEstimate(
            flops=2 * tokens * ff * dd, bytes_accessed=4 * ff * dd + 2 * tokens * (ff + dd), transcendentals=0
        ),
    )(all_hidden, all_grad)


def solution(mesh):
    nrow, ncol = mesh.shape["row"], mesh.shape["col"]

    nz, nx = nrow // 2, ncol // 2

    def shifted(value, axis, groups, d):
        pairs = [(g * 2 + o, (g + d) % groups * 2 + o) for g in range(groups) for o in range(2)]
        return lax.ppermute(value, axis, pairs)

    def on_device(hidden, down_weight, out_grad):
        *sums, all_hidden, all_grad = exchange(nrow, ncol, hidden, down_weight, out_grad)
        p_sums, early, h_sums = sums[:nz], sums[nz:-nx], sums[-nx:]
        h_total = h_sums[0]
        for d in range(1, nx):
            h_total += shifted(h_sums[d], "col", nx, d)
        p_total = p_sums[0]
        for d in range(1, nz):
            p_total += shifted(p_sums[d], "row", nz, d)
        p_total = jnp.concatenate([*early, p_total], axis=1)
        weight_grad = outer(all_hidden, all_grad)
        return p_total.astype(jnp.bfloat16), h_total.astype(jnp.bfloat16), weight_grad

    return jax.shard_map(
        on_device,
        mesh=mesh,
        in_specs=(P("col", "row"), P("row", "col"), P("row", "col")),
        out_specs=(P("row", "col"), P("col", "row"), P("row", "col")),
        check_vma=False,
    )
```
